32 devices in a mesh: row: 8 (over z, core), col: 4 (over y, x).
Axes of the slice: x: 2, y: 2, z: 4, core: 2. Of those that a mesh axis runs over, the one named last changes fastest.
Arguments:
- factor: bfloat16 [16, 1536, 6144], P(None, 'row'), may hold values from -0.078125 to 0.078125
- inverse_blocks: bfloat16 [4, 1536, 1536], P(None, 'row'), as said below
- right_side: float32 [16, 1536, 2048], P(None, 'row', 'col'), may hold values from -6 to 6
- shape_derivative: float32 [4, 1536, 2048], P(None, 'row', 'col')
Outputs:
- solved: float32 [4, 1536, 2048], P(None, 'row', 'col')
- trailing: float32 [12, 1536, 2048], P(None, 'row', 'col')
- sensitivity: float32 [4, 1536], P(None, 'row')
The draws below stay inside these ranges and needn't reach their ends.
Inputs may be any that keep to these rules, and one draw needn't show every extreme that they name: inverse_blocks[k] is the inverse supplied for the diagonal block of step k.
All inputs are finite; a program needn't handle non-finite values.
Results may differ from the reference program's by a relative error of at most 0.0045.
Values may be sent and summed in bfloat16 or wider, within the bound.
A program may use at most 128 MiB of HBM per device.

```python
import math
import jax
import jax.numpy as jnp
from jax import lax

NB = 1536
STEPS = 4
NBLK = 16
RHS = 2048
W = 6144


def draw_inverse_blocks(key, part):
    key_off = jax.random.fold_in(jax.random.fold_in(key, 11), 0)
    rough = jnp.clip(jax.random.normal(key_off, (STEPS, NB, NB), jnp.float32), -5.0, 5.0)
    diagonal_scale = jnp.ones((STEPS, NB, 1), jnp.float32)
    identity = (lax.broadcasted_iota(jnp.int32, (NB, NB), 0) == lax.broadcasted_iota(jnp.int32, (NB, NB), 1)).astype(jnp.float32)
    values = diagonal_scale * identity + 0.6 * rough / math.sqrt(NB)
    return values.astype(jnp.bfloat16)


def draw_shape_derivative(key, part):
    column = lax.broadcasted_iota(jnp.float32, (STEPS, NB, RHS), 2)
    key_val = jax.random.fold_in(key, 23)
    values = jnp.clip(jax.random.normal(key_val, (STEPS, NB, RHS), jnp.float32), -5.0, 5.0)
    ramp = 1.0 + 2.0 * column / (RHS - 1)
    return (values * ramp / math.sqrt(RHS)).astype(jnp.float32)


def block_scale(rng, dims, pieces, least, largest):
    loudness = 1.0
    for position, shards_of in pieces:
        heights = jax.random.uniform(jax.random.fold_in(jax.random.fold_in(rng, 6), position), (shards_of,), jnp.float32, least / len(pieces), largest / len(pieces))
        loudness = loudness * jnp.repeat(jnp.exp(heights), dims[position] // shards_of).reshape((-1,) + (1,) * (len(dims) - 1 - position))
    return loudness


def noise(key, shape, scale, limit, shards=(), kind=jnp.bfloat16):
    result = scale * jax.random.normal(key, shape, jnp.float32)
    if shards:
        result = result * block_scale(key, shape, shards, -0.22, 0.18)
    return jnp.clip(result, -limit, limit).astype(kind)


def setup_inputs(seed: int = 0) -> dict:
    key_of = jax.random.split(jax.random.key(seed), 5)
    factor = noise(key_of[0], (NBLK, NB, W), W ** -0.5, 0.078125, ((1, 8),))
    inverse_blocks = draw_inverse_blocks(jax.random.fold_in(key_of[4], 71), 0)
    right_side = noise(key_of[2], (NBLK, NB, RHS), 1.0, 6.0, ((1, 8), (2, 4)), jnp.float32)
    shape_derivative = draw_shape_derivative(jax.random.fold_in(key_of[4], 71), 0)
    return dict(factor=factor, inverse_blocks=inverse_blocks, right_side=right_side, shape_derivative=shape_derivative)


def reference(factor, inverse_blocks, right_side, shape_derivative):
    solved_list = []
    rounded_list = []
    for step in range(STEPS):
        residual = right_side[step]
        for earlier in range(step):
            panel = factor[step, :, earlier * NB:(earlier + 1) * NB]
            residual = residual - jnp.dot(panel, rounded_list[earlier], preferred_element_type=jnp.float32)
        residual_block = residual.astype(jnp.bfloat16)
        solution = jnp.dot(inverse_blocks[step], residual_block, preferred_element_type=jnp.float32)
        solved_list.append(solution)
        rounded_list.append(solution.astype(jnp.bfloat16))
    all_solved = jnp.concatenate(rounded_list, axis=0)
    trailing_list = []
    for block_row in range(STEPS, NBLK):
        product = jnp.dot(factor[block_row], all_solved, preferred_element_type=jnp.float32)
        trailing_list.append(right_side[block_row] - product)
    solved = jnp.stack(solved_list)
    trailing = jnp.stack(trailing_list)
    sensitivity = jnp.sum(solved * shape_derivative, axis=2)
    return solved, trailing, sensitivity
```

```python
import functools

import jax
import jax.numpy as jnp
from jax import lax
from jax.experimental import pallas as pl
from jax.experimental.pallas import tpu as pltpu
from jax.sharding import PartitionSpec as P

HALVES = 2
FULL_STEPS = 1
F32 = jnp.float32
BF16 = jnp.bfloat16
SIB, UP, DOWN = 0, 1, 2


def mm(a, b):
    return jnp.dot(a, b, preferred_element_type=F32)


def kernel(
    chips, peers,
    factor, inverse, right, deriv,
    solved_out, trailing_out, sens_out,
    panel, inv, end_inv, tail, racc, tacc, sd, sol, rbuf, xbuf, sacc, sens,
    load_sem, store_sem, end_sem, r_recv, x_recv, send_sem, peer_send, peer_recv,
):
    steps, rows, size = inv.shape
    halves, cols = racc.shape[0], racc.shape[3]
    blocks = tacc.shape[1]
    ranks = 2 * chips
    me = lax.axis_index("row")
    z = me // 2
    c = lax.rem(me, 2)
    other = 1 - c
    mine = lax.axis_index("col")
    last = chips - 1

    def low(k):
        return 0 if k < FULL_STEPS else 1

    loads = {}

    def load(name, src, dst):
        copy = pltpu.make_async_copy(src, dst, load_sem.at[len(loads)])
        copy.start()
        loads[name] = [copy, False]

    def ready(name):
        entry = loads[name]
        if not entry[1]:
            entry[0].wait()
            entry[1] = True

    def columns(h):
        return pl.ds(h * cols, cols)

    for h in range(halves):
        load(("r", h), right.at[pl.ds(0, steps), :, columns(h)], racc.at[h])

    def at_row(chip, core):
        return {"row": 2 * chip + core}

    barrier = pltpu.get_barrier_semaphore()

    def greet(chip, core):
        pl.semaphore_signal(
            barrier, inc=1, device_id=at_row(chip, core), device_id_type=pl.DeviceIdType.MESH
        )

    greet(z, other)
    for t in range(1, peers):
        pl.semaphore_signal(
            barrier, inc=1, device_id={"col": lax.rem(mine + t, peers)},
            device_id_type=pl.DeviceIdType.MESH,
        )
    pl.when(z > 0)(lambda: greet(z - 1, c))
    pl.when(z < last)(lambda: greet(z + 1, c))

    load(("inv", 0), inverse.at[0], inv.at[0])
    pairs = [(k, j) for j in range(steps) for k in range(j + 1, steps)]
    place = {pair: n for n, pair in enumerate(pairs)}
    for j in range(steps):
        for k in range(j + 1, steps):
            load(("panel", k, j), factor.at[k, :, pl.ds(j * size, size)], panel.at[place[k, j]])
        if j == 0:
            for h in range(halves):
                load(("d", h), deriv.at[:, :, columns(h)], sd.at[h])
            for h in range(halves):
                load(("t", h), right.at[pl.ds(steps, blocks), :, columns(h)], tacc.at[h])
        load(("tail", j), factor.at[pl.ds(steps, blocks), :, pl.ds(j * size, size)], tail.at[j])
        if j + 1 < steps:
            load(("inv", j + 1), inverse.at[j + 1], inv.at[j + 1])

    neighbours = jnp.where(z > 0, 1, 0) + jnp.where(z < last, 1, 0)
    pl.semaphore_wait(barrier, peers + neighbours)

    def shard(kind, k, h, index, direction):
        buffer, recv = (rbuf, r_recv) if kind == 0 else (xbuf, x_recv)
        chip, core = [(z, other), (z + 1, c), (z - 1, c)][direction]
        return pltpu.make_async_remote_copy(
            src_ref=buffer.at[k, h, index],
            dst_ref=buffer.at[k, h, index],
            send_sem=send_sem.at[kind, k, h, index, direction],
            recv_sem=recv.at[k, h, index],
            device_id=at_row(chip, core),
            device_id_type=pl.DeviceIdType.MESH,
        )

    def send(kind, k, h, chip, direction):
        shard(kind, k, h, 2 * chip + c, direction).start()

    def received(kind, k, h, chip, core):
        shard(kind, k, h, 2 * chip + core, SIB).wait_recv()

    def end_copy(k, target):
        n = k - FULL_STEPS
        return pltpu.make_async_remote_copy(
            src_ref=inverse.at[k], dst_ref=end_inv.at[n],
            send_sem=end_sem.at[0, n], recv_sem=end_sem.at[1, n],
            device_id=at_row(target, c), device_id_type=pl.DeviceIdType.MESH,
        )

    def send_own_r(k, h):
        lo = low(k)
        hi = last - lo
        pl.when(z + 1 <= hi)(lambda: send(0, k, h, z, UP))
        pl.when(z - 1 >= lo)(lambda: send(0, k, h, z, DOWN))
        pl.when((z >= lo) & (z <= hi))(lambda: send(0, k, h, z, SIB))

    def take_r(k, h):
        lo = low(k)
        hi = last - lo

        def gather():
            for t in range(1, chips):
                for d in (1, -1):
                    s = z - d * t

                    def arrive(s=s, d=d):
                        received(0, k, h, s, c)
                        onward = (z + 1 <= hi) if d == 1 else (z - 1 >= lo)
                        pl.when(onward)(lambda: send(0, k, h, s, UP if d == 1 else DOWN))
                        send(0, k, h, s, SIB)

                    pl.when((s >= 0) & (s <= last))(arrive)
            for s in range(chips):
                received(0, k, h, s, other)

        if lo == 0:
            gather()
        else:
            pl.when((z >= lo) & (z <= hi))(gather)

    def send_own_x(k, h, s):
        pl.when(z < last)(lambda: send(1, k, h, s, UP))
        pl.when(z > 0)(lambda: send(1, k, h, s, DOWN))
        send(1, k, h, s, SIB)

    def solve(k, h):
        lo = low(k)
        hi = last - lo
        ready(("inv", k))

        def own():
            gathered = rbuf[k, h].reshape(ranks * rows, cols)
            value = mm(inv[k], gathered)
            sol[h, k] = value
            xbuf[k, h, me] = value.astype(BF16)
            send_own_x(k, h, z)

        def for_end():
            n = k - FULL_STEPS
            if h == 0:
                end_copy(k, z).wait_recv()
            end = jnp.where(z == lo, 0, last)
            gathered = rbuf[k, h].reshape(ranks * rows, cols)
            xbuf[k, h, 2 * end + c] = mm(end_inv[n], gathered).astype(BF16)
            send_own_x(k, h, end)

        if lo == 0:
            own()
        else:
            pl.when((z >= lo) & (z <= hi))(own)
            pl.when((z == lo) | (z == hi))(for_end)

    def take_x(k, h):
        lo = low(k)
        hi = last - lo
        for t in range(1, chips):
            for d in (1, -1):
                home = z - d * t

                def arrive(s, d=d):
                    received(1, k, h, s, c)
                    onward = (z + 1 <= last) if d == 1 else (z - 1 >= 0)
                    pl.when(onward)(lambda: send(1, k, h, s, UP if d == 1 else DOWN))
                    send(1, k, h, s, SIB)

                pl.when((home >= lo) & (home <= hi))(lambda home=home, arrive=arrive: arrive(home))
                if lo == 1:
                    pl.when(home == lo)(lambda arrive=arrive: arrive(0))
                    pl.when(home == hi)(lambda arrive=arrive: arrive(last))
        for s in range(chips):
            received(1, k, h, s, other)
        if lo == 1:

            def widen():
                sol[h, k] = xbuf[k, h, me].astype(F32)

            pl.when((z < lo) | (z > hi))(widen)

    stores = []

    def store(src, dst):
        copy = pltpu.make_async_copy(src, dst, store_sem.at[len(stores)])
        copy.start()
        stores.append(copy)

    def spread(k, h):
        return xbuf[k, h].reshape(ranks * rows, cols)

    def next_r(k, h):
        ready(("panel", k + 1, k))
        value = racc[h, k + 1] - mm(panel[place[k + 1, k]], spread(k, h))
        rbuf[k + 1, h, me] = value.astype(BF16)
        send_own_r(k + 1, h)

    group = max(g for g in (4, 3, 2, 1) if blocks % g == 0)

    def finish(k, h):
        for m in range(k + 2, steps):
            ready(("panel", m, k))
            racc[h, m] -= mm(panel[place[m, k]], spread(k, h))
        ready(("t", h))
        ready(("tail", k))

        def update(i, carry):
            span = pl.ds(i * group, group)
            part = mm(tail[k, span].reshape(group * rows, size), spread(k, h))
            tacc[h, span] -= part.reshape(group, rows, cols)
            return carry

        lax.fori_loop(0, blocks // group, update, 0)
        if k == steps - 1:
            store(tacc.at[h], trailing_out.at[:, :, columns(h)])

    def sensitivity(k, h):
        ready(("d", h))
        store(sol.at[h, k], solved_out.at[k, :, columns(h)])
        part = jnp.sum(sol[h, k] * sd[h, k], axis=1, keepdims=True)
        lane = lax.broadcasted_iota(jnp.int32, (rows, 128), 1)
        sacc[...] += jnp.where(lane == k, part, 0.0)

    sacc[...] = jnp.zeros_like(sacc)
    for h in range(halves):
        ready(("r", h))
        rbuf[0, h, me] = racc[h, 0].astype(BF16)
        send_own_r(0, h)
    for k in range(FULL_STEPS, steps):
        pl.when(z == 0)(lambda k=k: end_copy(k, 1).start())
        pl.when(z == last)(lambda k=k: end_copy(k, last - 1).start())

    pending = None
    for k in range(steps):
        for h in range(halves):
            take_r(k, h)
            solve(k, h)
            if pending is not None:
                finish(*pending)
                sensitivity(*pending)
            take_x(k, h)
            if k + 1 < steps:
                next_r(k, h)
            pending = (k, h)
    sensitivity(*pending)
    sens[mine] = sacc[...]
    shares = []
    for t in range(1, peers):
        copy = pltpu.make_async_remote_copy(
            src_ref=sens.at[mine], dst_ref=sens.at[mine],
            send_sem=peer_send.at[t], recv_sem=peer_recv.at[t],
            device_id={"col": lax.rem(mine + t, peers)},
            device_id_type=pl.DeviceIdType.MESH,
        )
        copy.start()
        shares.append(copy)
    finish(*pending)
    for copy in shares:
        copy.wait()
    total = sens[0]
    for j in range(1, peers):
        total = total + sens[j]
    sens_out[...] = total

    def drain(n, carry):
        p = n // chips
        s = lax.rem(n, chips)
        k = p // halves
        h = lax.rem(p, halves)
        lo = jnp.where(k < FULL_STEPS, 0, 1)
        hi = last - lo
        home = jnp.clip(s, lo, hi)
        index = 2 * s + c

        def left(kind, direction):
            return lambda: shard(kind, k, h, index, direction).wait_send()

        pl.when((z >= lo) & (z <= hi))(left(0, SIB))
        pl.when((s <= z) & (z + 1 <= hi))(left(0, UP))
        pl.when((s >= z) & (z - 1 >= lo))(left(0, DOWN))
        left(1, SIB)()
        pl.when((home <= z) & (z + 1 <= last))(left(1, UP))
        pl.when((home >= z) & (z - 1 >= 0))(left(1, DOWN))
        return carry

    lax.fori_loop(0, steps * halves * chips, drain, 0)
    for k in range(FULL_STEPS, steps):
        pl.when((z == 0) | (z == last))(lambda k=k: end_copy(k, 1).wait_send())
    for copy in stores:
        copy.wait()


def local(chips, peers, factor, inverse_blocks, right_side, shape_derivative):
    steps, rows, size = inverse_blocks.shape
    blocks = factor.shape[0] - steps
    width = right_side.shape[2]
    cols = width // HALVES
    ranks = 2 * chips
    pairs = steps * (steps - 1) // 2
    ends = steps - FULL_STEPS
    multiplied = (pairs + steps * blocks) * rows * size * width + steps * rows * size * width
    anywhere = pl.BlockSpec(memory_space=pl.ANY)
    dma = pltpu.SemaphoreType.DMA
    solved, trailing, sens = pl.pallas_call(
        functools.partial(kernel, chips, peers),
        out_shape=(
            jax.ShapeDtypeStruct((steps, rows, width), F32),
            jax.ShapeDtypeStruct((blocks, rows, width), F32),
            jax.ShapeDtypeStruct((rows, 128), F32),
        ),
        in_specs=[anywhere] * 4,
        out_specs=(anywhere, anywhere, pl.BlockSpec(memory_space=pltpu.VMEM)),
        scratch_shapes=[
            pltpu.VMEM((pairs, rows, size), BF16),
            pltpu.VMEM((steps, rows, size), BF16),
            pltpu.VMEM((ends, rows, size), BF16),
            pltpu.VMEM((steps, blocks, rows, size), BF16),
            pltpu.VMEM((HALVES, steps, rows, cols), F32),
            pltpu.VMEM((HALVES, blocks, rows, cols), F32),
            pltpu.VMEM((HALVES, steps, rows, cols), F32),
            pltpu.VMEM((HALVES, steps, rows, cols), F32),
            pltpu.VMEM((steps, HALVES, ranks, rows, cols), BF16),
            pltpu.VMEM((steps, HALVES, ranks, rows, cols), BF16),
            pltpu.VMEM((rows, 128), F32),
            pltpu.VMEM((peers, rows, 128), F32),
            dma((pairs + 2 * steps + 3 * HALVES,)),
            dma((steps * HALVES + HALVES,)),
            dma((2, ends)),
            dma((steps, HALVES, ranks)),
            dma((steps, HALVES, ranks)),
            dma((2, steps, HALVES, ranks, 3)),
            dma((peers,)),
            dma((peers,)),
        ],
        compiler_params=pltpu.CompilerParams(
            collective_id=0, has_side_effects=True, vmem_limit_bytes=63 * 1024 * 1024
        ),
        cost_estimate=pl.CostEstimate(
            flops=2 * multiplied,
            bytes_accessed=2 * factor.size + 2 * inverse_blocks.size + 8 * right_side.size,
            transcendentals=0,
        ),
        name="substitution",
    )(factor, inverse_blocks, right_side, shape_derivative)
    return solved, trailing, sens[:, :steps].T


def solution(mesh):
    chips = mesh.shape["row"] // 2
    peers = mesh.shape["col"]
    return jax.shard_map(
        functools.partial(local, chips, peers),
        mesh=mesh,
        in_specs=(
            P(None, "row", None),
            P(None, "row", None),
            P(None, "row", "col"),
            P(None, "row", "col"),
        ),
        out_specs=(P(None, "row", "col"), P(None, "row", "col"), P(None, "row")),
        check_vma=False,
    )
```

```python
import functools

import jax
import jax.numpy as jnp
from jax import lax
from jax.experimental import pallas as pl
from jax.experimental.pallas import tpu as pltpu
from jax.sharding import PartitionSpec as P

HALVES = 2
FULL_STEPS = 1
F32 = jnp.float32
BF16 = jnp.bfloat16
SIB, UP, DOWN, FAR = 0, 1, 2, 3


def mm(a, b):
    return jnp.dot(a, b, preferred_element_type=F32)


def kernel(
    chips, peers,
    factor, inverse, right, deriv,
    solved_out, trailing_out, sens_out,
    panel, inv, end_inv, tail, racc, tacc, sd, sol, rbuf, xbuf, sacc, sens,
    load_sem, store_sem, end_sem, r_recv, x_recv, send_sem, share_sem, peer_send, peer_recv,
):
    steps, rows, size = inv.shape
    halves, cols = racc.shape[0], racc.shape[3]
    blocks = tacc.shape[1]
    ranks = 2 * chips
    me = lax.axis_index("row")
    z = me // 2
    c = lax.rem(me, 2)
    other = 1 - c
    mine = lax.axis_index("col")
    last = chips - 1

    def low(k):
        return 0 if k < FULL_STEPS else 1

    loads = {}

    def load(name, src, dst):
        copy = pltpu.make_async_copy(src, dst, load_sem.at[len(loads)])
        copy.start()
        loads[name] = [copy, False]

    def ready(name):
        entry = loads[name]
        if not entry[1]:
            entry[0].wait()
            entry[1] = True

    def columns(h):
        return pl.ds(h * cols, cols)

    for h in range(halves):
        load(("r", h), right.at[pl.ds(0, steps), :, columns(h)], racc.at[h])

    def at_row(chip, core):
        return {"row": 2 * chip + core}

    barrier = pltpu.get_barrier_semaphore()

    def greet(chip, core):
        pl.semaphore_signal(
            barrier, inc=1, device_id=at_row(chip, core), device_id_type=pl.DeviceIdType.MESH
        )

    greet(z, other)
    for t in range(1, peers):
        pl.semaphore_signal(
            barrier, inc=1, device_id={"col": lax.rem(mine + t, peers)},
            device_id_type=pl.DeviceIdType.MESH,
        )
    pl.when(z > 0)(lambda: greet(z - 1, c))
    pl.when(z < last)(lambda: greet(z + 1, c))
    pl.when((z == 0) | (z == last - 2))(lambda: greet(z + 2, c))
    pl.when((z == last) | (z == 2))(lambda: greet(z - 2, c))

    load(("inv", 0), inverse.at[0], inv.at[0])
    pairs = [(k, j) for j in range(steps) for k in range(j + 1, steps)]
    place = {pair: n for n, pair in enumerate(pairs)}
    for j in range(steps):
        for k in range(j + 1, steps):
            load(("panel", k, j), factor.at[k, :, pl.ds(j * size, size)], panel.at[place[k, j]])
        if j == 0:
            for h in range(halves):
                load(("d", h), deriv.at[:, :, columns(h)], sd.at[h])
            for h in range(halves):
                load(("t", h), right.at[pl.ds(steps, blocks), :, columns(h)], tacc.at[h])
        load(("tail", j), factor.at[pl.ds(steps, blocks), :, pl.ds(j * size, size)], tail.at[j])
        if j + 1 < steps:
            load(("inv", j + 1), inverse.at[j + 1], inv.at[j + 1])

    neighbours = jnp.where(z > 0, 1, 0) + jnp.where(z < last, 1, 0)
    neighbours += jnp.where((z == 0) | (z == last - 2), 1, 0)
    neighbours += jnp.where((z == last) | (z == 2), 1, 0)
    pl.semaphore_wait(barrier, peers + neighbours)

    def shard(kind, k, h, index, direction):
        buffer, recv = (rbuf, r_recv) if kind == 0 else (xbuf, x_recv)
        far = jnp.where(z == 0, 2, last - 2)
        chip, core = [(z, other), (z + 1, c), (z - 1, c), (far, c)][direction]
        return pltpu.make_async_remote_copy(
            src_ref=buffer.at[k, h, index],
            dst_ref=buffer.at[k, h, index],
            send_sem=send_sem.at[kind, k, h, index, direction],
            recv_sem=recv.at[k, h, index],
            device_id=at_row(chip, core),
            device_id_type=pl.DeviceIdType.MESH,
        )

    def send(kind, k, h, chip, direction):
        shard(kind, k, h, 2 * chip + c, direction).start()

    def received(kind, k, h, chip, core):
        shard(kind, k, h, 2 * chip + core, SIB).wait_recv()

    sharers = max(
        g for g in range(1, peers + 1) if peers % g == 0 and rows % g == 0 and rows // g % 16 == 0
    )
    part_rows = rows // sharers
    turn = lax.rem(mine, sharers)
    piece = pl.ds(pl.multiple_of(turn * part_rows, part_rows), part_rows)

    def share(k, t):
        n = k - FULL_STEPS
        return pltpu.make_async_remote_copy(
            src_ref=end_inv.at[n, piece], dst_ref=end_inv.at[n, piece],
            send_sem=share_sem.at[0, n, t], recv_sem=share_sem.at[1, n, t],
            device_id={"col": mine - turn + lax.rem(turn + t, sharers)},
            device_id_type=pl.DeviceIdType.MESH,
        )

    def share_end(k):
        def go():
            end_copy(k, z).wait_recv()
            for t in range(1, sharers):
                share(k, t).start()

        pl.when((z == 1) | (z == last - 1))(go)

    def end_copy(k, target):
        n = k - FULL_STEPS
        return pltpu.make_async_remote_copy(
            src_ref=inverse.at[k, piece], dst_ref=end_inv.at[n, piece],
            send_sem=end_sem.at[0, n], recv_sem=end_sem.at[1, n],
            device_id=at_row(target, c), device_id_type=pl.DeviceIdType.MESH,
        )

    def send_own_r(k, h):
        lo = low(k)
        hi = last - lo
        pl.when(z + 1 <= hi)(lambda: send(0, k, h, z, UP))
        pl.when(z - 1 >= lo)(lambda: send(0, k, h, z, DOWN))
        if lo == 0:
            send(0, k, h, z, SIB)
        else:
            pl.when((z >= lo) & (z <= hi))(lambda: send(0, k, h, z, SIB))
            pl.when((z == 0) | (z == last))(lambda: send(0, k, h, z, FAR))

    def take_r(k, h):
        lo = low(k)
        hi = last - lo

        def gather():
            for t in range(1, chips):
                for d in (1, -1):
                    s = z - d * t

                    def arrive(s=s, d=d):
                        received(0, k, h, s, c)
                        onward = (z + 1 <= hi) if d == 1 else (z - 1 >= lo)
                        if lo == 1:
                            onward &= ((s > 0) | (z > 1)) if d == 1 else ((s < last) | (z < last - 1))
                        pl.when(onward)(lambda: send(0, k, h, s, UP if d == 1 else DOWN))
                        send(0, k, h, s, SIB)

                    pl.when((s >= 0) & (s <= last))(arrive)
            for s in range(chips):
                received(0, k, h, s, other)

        if lo == 0:
            gather()
        else:
            pl.when((z >= lo) & (z <= hi))(gather)

    def send_own_x(k, h, s):
        pl.when(z < last)(lambda: send(1, k, h, s, UP))
        pl.when(z > 0)(lambda: send(1, k, h, s, DOWN))
        send(1, k, h, s, SIB)

    def solve(k, h):
        lo = low(k)
        hi = last - lo
        ready(("inv", k))

        def own():
            gathered = rbuf[k, h].reshape(ranks * rows, cols)
            value = mm(inv[k], gathered)
            sol[h, k] = value
            xbuf[k, h, me] = value.astype(BF16)
            send_own_x(k, h, z)

        def for_end():
            n = k - FULL_STEPS
            if h == 0:
                for t in range(1, sharers):
                    share(k, t).wait_recv()
            end = jnp.where(z == lo, 0, last)
            gathered = rbuf[k, h].reshape(ranks * rows, cols)
            xbuf[k, h, 2 * end + c] = mm(end_inv[n], gathered).astype(BF16)
            send_own_x(k, h, end)

        if lo == 0:
            own()
        else:
            pl.when((z >= lo) & (z <= hi))(own)
            pl.when((z == lo) | (z == hi))(for_end)

    def take_x(k, h):
        lo = low(k)
        hi = last - lo
        for t in range(1, chips):
            for d in (1, -1):
                home = z - d * t

                def arrive(s, d=d):
                    received(1, k, h, s, c)
                    onward = (z + 1 <= last) if d == 1 else (z - 1 >= 0)
                    pl.when(onward)(lambda: send(1, k, h, s, UP if d == 1 else DOWN))
                    send(1, k, h, s, SIB)

                pl.when((home >= lo) & (home <= hi))(lambda home=home, arrive=arrive: arrive(home))
                if lo == 1:
                    pl.when(home == lo)(lambda arrive=arrive: arrive(0))
                    pl.when(home == hi)(lambda arrive=arrive: arrive(last))
        for s in range(chips):
            received(1, k, h, s, other)
        if lo == 1:

            def widen():
                sol[h, k] = xbuf[k, h, me].astype(F32)

            pl.when((z < lo) | (z > hi))(widen)

    stores = []

    def store(src, dst):
        copy = pltpu.make_async_copy(src, dst, store_sem.at[len(stores)])
        copy.start()
        stores.append(copy)

    def spread(k, h):
        return xbuf[k, h].reshape(ranks * rows, cols)

    def next_r(k, h):
        ready(("panel", k + 1, k))
        value = racc[h, k + 1] - mm(panel[place[k + 1, k]], spread(k, h))
        rbuf[k + 1, h, me] = value.astype(BF16)
        send_own_r(k + 1, h)

    group = max(g for g in (4, 3, 2, 1) if blocks % g == 0)

    def finish(k, h):
        for m in range(k + 2, steps):
            ready(("panel", m, k))
            racc[h, m] -= mm(panel[place[m, k]], spread(k, h))
        ready(("t", h))
        ready(("tail", k))

        def update(i, carry):
            span = pl.ds(i * group, group)
            part = mm(tail[k, span].reshape(group * rows, size), spread(k, h))
            tacc[h, span] -= part.reshape(group, rows, cols)
            return carry

        lax.fori_loop(0, blocks // group, update, 0)
        if k == steps - 1:
            store(tacc.at[h], trailing_out.at[:, :, columns(h)])

    def sensitivity(k, h):
        ready(("d", h))
        store(sol.at[h, k], solved_out.at[k, :, columns(h)])
        part = jnp.sum(sol[h, k] * sd[h, k], axis=1, keepdims=True)
        lane = lax.broadcasted_iota(jnp.int32, (rows, 128), 1)
        sacc[...] += jnp.where(lane == k, part, 0.0)

    sacc[...] = jnp.zeros_like(sacc)
    for h in range(halves):
        ready(("r", h))
        rbuf[0, h, me] = racc[h, 0].astype(BF16)
        send_own_r(0, h)
    for k in range(FULL_STEPS, steps):
        pl.when(z == 0)(lambda k=k: end_copy(k, 1).start())
        pl.when(z == last)(lambda k=k: end_copy(k, last - 1).start())

    pending = []
    for k in range(steps):
        for h in range(halves):
            take_r(k, h)
            solve(k, h)
        if k == 0:
            share_end(FULL_STEPS)
        for h in range(halves):
            if pending:
                finish(*pending[h])
                sensitivity(*pending[h])
            take_x(k, h)
            if k + 1 < steps:
                next_r(k, h)
        if k == 0:
            for n in range(FULL_STEPS + 1, steps):
                share_end(n)
        pending = [(k, h) for h in range(halves)]
    for phase in pending:
        sensitivity(*phase)
    sens[mine] = sacc[...]
    shares = []
    for t in range(1, peers):
        copy = pltpu.make_async_remote_copy(
            src_ref=sens.at[mine], dst_ref=sens.at[mine],
            send_sem=peer_send.at[t], recv_sem=peer_recv.at[t],
            device_id={"col": lax.rem(mine + t, peers)},
            device_id_type=pl.DeviceIdType.MESH,
        )
        copy.start()
        shares.append(copy)
    for phase in pending:
        finish(*phase)
    for copy in shares:
        copy.wait()
    total = sens[0]
    for j in range(1, peers):
        total = total + sens[j]
    sens_out[...] = total

    def drain(n, carry):
        p = n // chips
        s = lax.rem(n, chips)
        k = p // halves
        h = lax.rem(p, halves)
        lo = jnp.where(k < FULL_STEPS, 0, 1)
        hi = last - lo
        home = jnp.clip(s, lo, hi)
        index = 2 * s + c

        def left(kind, direction):
            return lambda: shard(kind, k, h, index, direction).wait_send()

        pl.when((z >= lo) & (z <= hi))(left(0, SIB))
        skip_up = (lo == 1) & (s == 0) & (z == 1)
        skip_down = (lo == 1) & (s == last) & (z == last - 1)
        pl.when((s <= z) & (z + 1 <= hi) & jnp.logical_not(skip_up))(left(0, UP))
        pl.when((s >= z) & (z - 1 >= lo) & jnp.logical_not(skip_down))(left(0, DOWN))
        pl.when((lo == 1) & (s == z) & ((z == 0) | (z == last)))(left(0, FAR))
        left(1, SIB)()
        pl.when((home <= z) & (z + 1 <= last))(left(1, UP))
        pl.when((home >= z) & (z - 1 >= 0))(left(1, DOWN))
        return carry

    lax.fori_loop(0, steps * halves * chips, drain, 0)
    for k in range(FULL_STEPS, steps):
        pl.when((z == 0) | (z == last))(lambda k=k: end_copy(k, 1).wait_send())

        def left_share(k=k):
            for t in range(1, sharers):
                share(k, t).wait_send()

        pl.when((z == 1) | (z == last - 1))(left_share)
    for copy in stores:
        copy.wait()


def local(chips, peers, factor, inverse_blocks, right_side, shape_derivative):
    steps, rows, size = inverse_blocks.shape
    blocks = factor.shape[0] - steps
    width = right_side.shape[2]
    cols = width // HALVES
    ranks = 2 * chips
    pairs = steps * (steps - 1) // 2
    ends = steps - FULL_STEPS
    multiplied = (pairs + steps * blocks) * rows * size * width + steps * rows * size * width
    anywhere = pl.BlockSpec(memory_space=pl.ANY)
    dma = pltpu.SemaphoreType.DMA
    solved, trailing, sens = pl.pallas_call(
        functools.partial(kernel, chips, peers),
        out_shape=(
            jax.ShapeDtypeStruct((steps, rows, width), F32),
            jax.ShapeDtypeStruct((blocks, rows, width), F32),
            jax.ShapeDtypeStruct((rows, 128), F32),
        ),
        in_specs=[anywhere] * 4,
        out_specs=(anywhere, anywhere, pl.BlockSpec(memory_space=pltpu.VMEM)),
        scratch_shapes=[
            pltpu.VMEM((pairs, rows, size), BF16),
            pltpu.VMEM((steps, rows, size), BF16),
            pltpu.VMEM((ends, rows, size), BF16),
            pltpu.VMEM((steps, blocks, rows, size), BF16),
            pltpu.VMEM((HALVES, steps, rows, cols), F32),
            pltpu.VMEM((HALVES, blocks, rows, cols), F32),
            pltpu.VMEM((HALVES, steps, rows, cols), F32),
            pltpu.VMEM((HALVES, steps, rows, cols), F32),
            pltpu.VMEM((steps, HALVES, ranks, rows, cols), BF16),
            pltpu.VMEM((steps, HALVES, ranks, rows, cols), BF16),
            pltpu.VMEM((rows, 128), F32),
            pltpu.VMEM((peers, rows, 128), F32),
            dma((pairs + 2 * steps + 3 * HALVES,)),
            dma((steps * HALVES + HALVES,)),
            dma((2, ends)),
            dma((steps, HALVES, ranks)),
            dma((steps, HALVES, ranks)),
            dma((2, steps, HALVES, ranks, 4)),
            dma((2, ends, peers)),
            dma((peers,)),
            dma((peers,)),
        ],
        compiler_params=pltpu.CompilerParams(
            collective_id=0, has_side_effects=True, vmem_limit_bytes=63 * 1024 * 1024
        ),
        cost_estimate=pl.CostEstimate(
            flops=2 * multiplied,
            bytes_accessed=2 * factor.size + 2 * inverse_blocks.size + 8 * right_side.size,
            transcendentals=0,
        ),
        name="substitution",
    )(factor, inverse_blocks, right_side, shape_derivative)
    return solved, trailing, sens[:, :steps].T


def solution(mesh):
    chips = mesh.shape["row"] // 2
    peers = mesh.shape["col"]
    return jax.shard_map(
        functools.partial(local, chips, peers),
        mesh=mesh,
        in_specs=(
            P(None, "row", None),
            P(None, "row", None),
            P(None, "row", "col"),
            P(None, "row", "col"),
        ),
        out_specs=(P(None, "row", "col"), P(None, "row", "col"), P(None, "row")),
        check_vma=False,
    )
```

```python
import functools

import jax
import jax.numpy as jnp
from jax import lax
from jax.experimental import pallas as pl
from jax.experimental.pallas import tpu as pltpu
from jax.sharding import PartitionSpec as P

HALVES = 2
FULL_STEPS = 1
F32 = jnp.float32
BF16 = jnp.bfloat16
SIB, UP, DOWN, FAR = 0, 1, 2, 3


def mm(a, b):
    return jnp.dot(a, b, preferred_element_type=F32)


def kernel(
    chips, peers,
    factor, inverse, right, deriv,
    solved_out, part_out, last_out, sens_out,
    panel, inv, end_inv, tail, racc, tacc, sd, sol, rbuf, xbuf, sacc, sens,
    load_sem, store_sem, end_sem, r_recv, x_recv, send_sem, share_sem, peer_send, peer_recv,
):
    steps, rows, size = inv.shape
    halves, cols = racc.shape[0], racc.shape[3]
    blocks = tacc.shape[1]
    ranks = 2 * chips
    me = lax.axis_index("row")
    z = me // 2
    c = lax.rem(me, 2)
    other = 1 - c
    mine = lax.axis_index("col")
    last = chips - 1

    def low(k):
        return 0 if k < FULL_STEPS else 1

    loads = {}

    def load(name, src, dst):
        copy = pltpu.make_async_copy(src, dst, load_sem.at[len(loads)])
        copy.start()
        loads[name] = [copy, False]

    def ready(name):
        entry = loads[name]
        if not entry[1]:
            entry[0].wait()
            entry[1] = True

    def columns(h):
        return pl.ds(h * cols, cols)

    for h in range(halves):
        load(("r", h), right.at[pl.ds(0, steps), :, columns(h)], racc.at[h])

    def at_row(chip, core):
        return {"row": 2 * chip + core}

    barrier = pltpu.get_barrier_semaphore()

    def greet(chip, core):
        pl.semaphore_signal(
            barrier, inc=1, device_id=at_row(chip, core), device_id_type=pl.DeviceIdType.MESH
        )

    greet(z, other)
    for t in range(1, peers):
        pl.semaphore_signal(
            barrier, inc=1, device_id={"col": lax.rem(mine + t, peers)},
            device_id_type=pl.DeviceIdType.MESH,
        )
    pl.when(z > 0)(lambda: greet(z - 1, c))
    pl.when(z < last)(lambda: greet(z + 1, c))
    pl.when((z == 0) | (z == last - 2))(lambda: greet(z + 2, c))
    pl.when((z == last) | (z == 2))(lambda: greet(z - 2, c))

    load(("inv", 0), inverse.at[0], inv.at[0])
    pairs = [(k, j) for j in range(steps) for k in range(j + 1, steps)]
    place = {pair: n for n, pair in enumerate(pairs)}
    for j in range(steps):
        for k in range(j + 1, steps):
            load(("panel", k, j), factor.at[k, :, pl.ds(j * size, size)], panel.at[place[k, j]])
        if j == 0:
            for h in range(halves):
                load(("d", h), deriv.at[:, :, columns(h)], sd.at[h])
            for h in range(halves):
                load(("t", h), right.at[pl.ds(steps, blocks), :, columns(h)], tacc.at[h])
        load(("tail", j), factor.at[pl.ds(steps, blocks), :, pl.ds(j * size, size)], tail.at[j])
        if j + 1 < steps:
            load(("inv", j + 1), inverse.at[j + 1], inv.at[j + 1])

    neighbours = jnp.where(z > 0, 1, 0) + jnp.where(z < last, 1, 0)
    neighbours += jnp.where((z == 0) | (z == last - 2), 1, 0)
    neighbours += jnp.where((z == last) | (z == 2), 1, 0)
    pl.semaphore_wait(barrier, peers + neighbours)

    def shard(kind, k, h, index, direction):
        buffer, recv = (rbuf, r_recv) if kind == 0 else (xbuf, x_recv)
        far = jnp.where(z == 0, 2, last - 2)
        chip, core = [(z, other), (z + 1, c), (z - 1, c), (far, c)][direction]
        return pltpu.make_async_remote_copy(
            src_ref=buffer.at[k, h, index],
            dst_ref=buffer.at[k, h, index],
            send_sem=send_sem.at[kind, k, h, index, direction],
            recv_sem=recv.at[k, h, index],
            device_id=at_row(chip, core),
            device_id_type=pl.DeviceIdType.MESH,
        )

    def send(kind, k, h, chip, direction):
        shard(kind, k, h, 2 * chip + c, direction).start()

    def received(kind, k, h, chip, core):
        shard(kind, k, h, 2 * chip + core, SIB).wait_recv()

    sharers = max(
        g for g in range(1, peers + 1) if peers % g == 0 and rows % g == 0 and rows // g % 16 == 0
    )
    part_rows = rows // sharers
    turn = lax.rem(mine, sharers)
    piece = pl.ds(pl.multiple_of(turn * part_rows, part_rows), part_rows)

    def share(k, t):
        n = k - FULL_STEPS
        return pltpu.make_async_remote_copy(
            src_ref=end_inv.at[n, piece], dst_ref=end_inv.at[n, piece],
            send_sem=share_sem.at[0, n, t], recv_sem=share_sem.at[1, n, t],
            device_id={"col": mine - turn + lax.rem(turn + t, sharers)},
            device_id_type=pl.DeviceIdType.MESH,
        )

    def share_end(k):
        def go():
            end_copy(k, z).wait_recv()
            for t in range(1, sharers):
                share(k, t).start()

        pl.when((z == 1) | (z == last - 1))(go)

    def end_copy(k, target):
        n = k - FULL_STEPS
        return pltpu.make_async_remote_copy(
            src_ref=inverse.at[k, piece], dst_ref=end_inv.at[n, piece],
            send_sem=end_sem.at[0, n], recv_sem=end_sem.at[1, n],
            device_id=at_row(target, c), device_id_type=pl.DeviceIdType.MESH,
        )

    def send_own_r(k, h):
        lo = low(k)
        hi = last - lo
        pl.when(z + 1 <= hi)(lambda: send(0, k, h, z, UP))
        pl.when(z - 1 >= lo)(lambda: send(0, k, h, z, DOWN))
        if lo == 0:
            send(0, k, h, z, SIB)
        else:
            pl.when((z >= lo) & (z <= hi))(lambda: send(0, k, h, z, SIB))
            pl.when((z == 0) | (z == last))(lambda: send(0, k, h, z, FAR))

    def take_r(k, h):
        lo = low(k)
        hi = last - lo

        def gather():
            for t in range(1, chips):
                for d in (1, -1):
                    s = z - d * t

                    def arrive(s=s, d=d):
                        received(0, k, h, s, c)
                        onward = (z + 1 <= hi) if d == 1 else (z - 1 >= lo)
                        if lo == 1:
                            onward &= ((s > 0) | (z > 1)) if d == 1 else ((s < last) | (z < last - 1))
                        pl.when(onward)(lambda: send(0, k, h, s, UP if d == 1 else DOWN))
                        send(0, k, h, s, SIB)

                    pl.when((s >= 0) & (s <= last))(arrive)
            for s in range(chips):
                received(0, k, h, s, other)

        if lo == 0:
            gather()
        else:
            pl.when((z >= lo) & (z <= hi))(gather)

    def send_own_x(k, h, s):
        pl.when(z < last)(lambda: send(1, k, h, s, UP))
        pl.when(z > 0)(lambda: send(1, k, h, s, DOWN))
        send(1, k, h, s, SIB)

    def solve(k, h):
        lo = low(k)
        hi = last - lo
        ready(("inv", k))

        def own():
            gathered = rbuf[k, h].reshape(ranks * rows, cols)
            value = mm(inv[k], gathered)
            sol[h, k] = value
            xbuf[k, h, me] = value.astype(BF16)
            send_own_x(k, h, z)

        def for_end():
            n = k - FULL_STEPS
            if h == 0:
                for t in range(1, sharers):
                    share(k, t).wait_recv()
            end = jnp.where(z == lo, 0, last)
            gathered = rbuf[k, h].reshape(ranks * rows, cols)
            xbuf[k, h, 2 * end + c] = mm(end_inv[n], gathered).astype(BF16)
            send_own_x(k, h, end)

        if lo == 0:
            own()
        else:
            pl.when((z >= lo) & (z <= hi))(own)
            pl.when((z == lo) | (z == hi))(for_end)

    def take_x(k, h):
        lo = low(k)
        hi = last - lo
        for t in range(1, chips):
            for d in (1, -1):
                home = z - d * t

                def arrive(s, d=d):
                    received(1, k, h, s, c)
                    onward = (z + 1 <= last) if d == 1 else (z - 1 >= 0)
                    pl.when(onward)(lambda: send(1, k, h, s, UP if d == 1 else DOWN))
                    send(1, k, h, s, SIB)

                pl.when((home >= lo) & (home <= hi))(lambda home=home, arrive=arrive: arrive(home))
                if lo == 1:
                    pl.when(home == lo)(lambda arrive=arrive: arrive(0))
                    pl.when(home == hi)(lambda arrive=arrive: arrive(last))
        for s in range(chips):
            received(1, k, h, s, other)
        if lo == 1:

            def widen():
                sol[h, k] = xbuf[k, h, me].astype(F32)

            pl.when((z < lo) | (z > hi))(widen)

    stores = []

    def store(src, dst):
        copy = pltpu.make_async_copy(src, dst, store_sem.at[len(stores)])
        copy.start()
        stores.append(copy)

    def spread(k, h):
        return xbuf[k, h].reshape(ranks * rows, cols)

    def next_r(k, h):
        ready(("panel", k + 1, k))
        value = racc[h, k + 1] - mm(panel[place[k + 1, k]], spread(k, h))
        rbuf[k + 1, h, me] = value.astype(BF16)
        send_own_r(k + 1, h)

    group = max(g for g in (4, 3, 2, 1) if blocks % g == 0)

    def finish(k, h):
        for m in range(k + 2, steps):
            ready(("panel", m, k))
            racc[h, m] -= mm(panel[place[m, k]], spread(k, h))
        ready(("t", h))
        ready(("tail", k))

        def update(i, carry):
            span = pl.ds(i * group, group)
            part = mm(tail[k, span].reshape(group * rows, size), spread(k, h))
            tacc[h, span] -= part.reshape(group, rows, cols)
            return carry

        lax.fori_loop(0, blocks // group, update, 0)
        if k == steps - (2 if h == halves - 1 else 1):
            store(tacc.at[h], part_out.at[:, :, columns(h)])

    def sensitivity(k, h):
        ready(("d", h))
        store(sol.at[h, k], solved_out.at[k, :, columns(h)])
        part = jnp.sum(sol[h, k] * sd[h, k], axis=1, keepdims=True)
        lane = lax.broadcasted_iota(jnp.int32, (rows, 128), 1)
        sacc[pl.ds(0, rows)] += jnp.where(lane == k, part, 0.0)

    def drain(k, n, carry):
        h = n // chips
        s = lax.rem(n, chips)
        lo = jnp.int32(low(k))
        hi = last - lo
        home = jnp.clip(s, lo, hi)
        index = 2 * s + c

        def left(kind, direction):
            return lambda: shard(kind, k, h, index, direction).wait_send()

        pl.when((z >= lo) & (z <= hi))(left(0, SIB))
        skip_up = (lo == 1) & (s == 0) & (z == 1)
        skip_down = (lo == 1) & (s == last) & (z == last - 1)
        pl.when((s <= z) & (z + 1 <= hi) & jnp.logical_not(skip_up))(left(0, UP))
        pl.when((s >= z) & (z - 1 >= lo) & jnp.logical_not(skip_down))(left(0, DOWN))
        pl.when((lo == 1) & (s == z) & ((z == 0) | (z == last)))(left(0, FAR))
        left(1, SIB)()
        pl.when((home <= z) & (z + 1 <= last))(left(1, UP))
        pl.when((home >= z) & (z - 1 >= 0))(left(1, DOWN))
        return carry

    def drain_step(k):
        lax.fori_loop(0, halves * chips, functools.partial(drain, k), 0)

    sacc[...] = jnp.zeros_like(sacc)
    for h in range(halves):
        ready(("r", h))
        rbuf[0, h, me] = racc[h, 0].astype(BF16)
        send_own_r(0, h)
    for k in range(FULL_STEPS, steps):
        pl.when(z == 0)(lambda k=k: end_copy(k, 1).start())
        pl.when(z == last)(lambda k=k: end_copy(k, last - 1).start())

    pending = []
    for k in range(steps):
        for h in range(halves):
            take_r(k, h)
            solve(k, h)
        if k == 0:
            share_end(FULL_STEPS)
        else:
            drain_step(k - 1)
        for h in range(halves):
            if k == steps - 1 and h > 0:
                finish(k, h - 1)
            for phase in pending[h:] if k < steps - 1 or h == 0 else []:
                finish(*phase)
                sensitivity(*phase)
                if k < steps - 1:
                    break
            take_x(k, h)
            if k + 1 < steps:
                next_r(k, h)
            else:
                if h == halves - 1:
                    store(xbuf.at[k, h], last_out)
                sensitivity(k, h)
        if k == 0:
            for n in range(FULL_STEPS + 1, steps):
                share_end(n)
        pending = [(k, h) for h in range(halves)]
    sens[mine] = sacc[...].T[: sens.shape[1]]
    shares = []
    for t in range(1, peers):
        copy = pltpu.make_async_remote_copy(
            src_ref=sens.at[mine], dst_ref=sens.at[mine],
            send_sem=peer_send.at[t], recv_sem=peer_recv.at[t],
            device_id={"col": lax.rem(mine + t, peers)},
            device_id_type=pl.DeviceIdType.MESH,
        )
        copy.start()
        shares.append(copy)
    drain_step(steps - 1)
    for copy in shares:
        copy.wait()
    total = sens[0]
    for j in range(1, peers):
        total = total + sens[j]
    sens_out[...] = total

    for k in range(FULL_STEPS, steps):
        pl.when((z == 0) | (z == last))(lambda k=k: end_copy(k, 1).wait_send())

        def left_share(k=k):
            for t in range(1, sharers):
                share(k, t).wait_send()

        pl.when((z == 1) | (z == last - 1))(left_share)
    for copy in stores:
        copy.wait()


def last_kernel(tail, spread, part, solved, trailing_out, solved_out):
    blocks, rows, size = tail.shape
    product = mm(tail[...].reshape(blocks * rows, size), spread[...].reshape(size, spread.shape[2]))
    done = part.shape[2] - spread.shape[2]
    trailing_out[:, :, :done] = part[:, :, :done]
    trailing_out[:, :, done:] = part[:, :, done:] - product.reshape(blocks, rows, spread.shape[2])
    solved_out[...] = solved[...]


def add_last(factor, spread, part, solved):
    steps, rows, width = solved.shape
    blocks = part.shape[0]
    size = spread.shape[0] * rows
    group = 2 if steps % 2 == 0 and blocks % 2 == 0 else 1
    final = steps // group - 1
    one = lambda i: (i, 0, 0)
    kept = lambda i: (jnp.minimum(i, final), 0, 0)
    wide = (group, rows, width)
    return pl.pallas_call(
        last_kernel,
        grid=(blocks // group,),
        in_specs=[
            pl.BlockSpec((group, rows, size), lambda i: (steps // group + i, 0, steps - 1)),
            pl.BlockSpec(spread.shape, lambda i: (0, 0, 0)),
            pl.BlockSpec(wide, one),
            pl.BlockSpec(wide, kept),
        ],
        out_specs=(pl.BlockSpec(wide, one), pl.BlockSpec(wide, kept)),
        out_shape=(
            jax.ShapeDtypeStruct(part.shape, F32), jax.ShapeDtypeStruct(solved.shape, F32)
        ),
        compiler_params=pltpu.CompilerParams(vmem_limit_bytes=63 * 1024 * 1024),
        cost_estimate=pl.CostEstimate(
            flops=2 * blocks * rows * size * spread.shape[2],
            bytes_accessed=2 * blocks * rows * size + 8 * part.size + 8 * solved.size,
            transcendentals=0,
        ),
        name="last_block",
    )(factor, spread, part, solved)[::-1]


def local(chips, peers, factor, inverse_blocks, right_side, shape_derivative):
    steps, rows, size = inverse_blocks.shape
    blocks = factor.shape[0] - steps
    width = right_side.shape[2]
    cols = width // HALVES
    ranks = 2 * chips
    pairs = steps * (steps - 1) // 2
    ends = steps - FULL_STEPS
    padded = -(-rows // 128) * 128
    lines = -(-steps // 8) * 8
    early = steps - 1
    multiplied = (pairs + early * blocks + steps) * rows * size * width
    anywhere = pl.BlockSpec(memory_space=pl.ANY)
    dma = pltpu.SemaphoreType.DMA
    solved, part, spread, sens = pl.pallas_call(
        functools.partial(kernel, chips, peers),
        out_shape=(
            jax.ShapeDtypeStruct((steps, rows, width), F32),
            jax.ShapeDtypeStruct((blocks, rows, width), F32),
            jax.ShapeDtypeStruct((ranks, rows, cols), BF16),
            jax.ShapeDtypeStruct((lines, padded), F32),
        ),
        in_specs=[anywhere] * 4,
        out_specs=(anywhere, anywhere, anywhere, pl.BlockSpec(memory_space=pltpu.VMEM)),
        scratch_shapes=[
            pltpu.VMEM((pairs, rows, size), BF16),
            pltpu.VMEM((steps, rows, size), BF16),
            pltpu.VMEM((ends, rows, size), BF16),
            pltpu.VMEM((steps, blocks, rows, size), BF16),
            pltpu.VMEM((HALVES, steps, rows, cols), F32),
            pltpu.VMEM((HALVES, blocks, rows, cols), F32),
            pltpu.VMEM((HALVES, steps, rows, cols), F32),
            pltpu.VMEM((HALVES, steps, rows, cols), F32),
            pltpu.VMEM((steps, HALVES, ranks, rows, cols), BF16),
            pltpu.VMEM((steps, HALVES, ranks, rows, cols), BF16),
            pltpu.VMEM((padded, 128), F32),
            pltpu.VMEM((peers, lines, padded), F32),
            dma((pairs + 2 * steps + 3 * HALVES,)),
            dma((steps * HALVES + HALVES + 1,)),
            dma((2, ends)),
            dma((steps, HALVES, ranks)),
            dma((steps, HALVES, ranks)),
            dma((2, steps, HALVES, ranks, 4)),
            dma((2, ends, peers)),
            dma((peers,)),
            dma((peers,)),
        ],
        compiler_params=pltpu.CompilerParams(
            collective_id=0, has_side_effects=True, vmem_limit_bytes=63 * 1024 * 1024
        ),
        cost_estimate=pl.CostEstimate(
            flops=2 * multiplied,
            bytes_accessed=2 * factor.size + 2 * inverse_blocks.size + 8 * right_side.size,
            transcendentals=0,
        ),
        name="substitution",
    )(factor, inverse_blocks, right_side, shape_derivative)
    solved, trailing = add_last(factor, spread, part, solved)
    return solved, trailing, sens[:steps, :rows]


def solution(mesh):
    chips = mesh.shape["row"] // 2
    peers = mesh.shape["col"]
    return jax.shard_map(
        functools.partial(local, chips, peers),
        mesh=mesh,
        in_specs=(
            P(None, "row", None),
            P(None, "row", None),
            P(None, "row", "col"),
            P(None, "row", "col"),
        ),
        out_specs=(P(None, "row", "col"), P(None, "row", "col"), P(None, "row")),
        check_vma=False,
    )
```
